32 devices in a mesh: parts: 1, layer: 2 (over core), width: 16 (over z, y, x).
Axes of the slice: x: 2, y: 2, z: 4, core: 2. Of those that a mesh axis runs over, the one named last changes fastest.
Arguments:
- src_ids: int32 [2, 8192, 128], P('layer', ('parts', 'width')), may hold values from 0 to 1023, as said below
- src_acts: bfloat16 [2, 8192, 128], P('layer', ('parts', 'width')), may hold values from 0.099609375 to 4
- tgt_ids: int32 [2, 8192, 128], P(None, ('parts', 'width')), may hold values from 0 to 1023, as said below
- tgt_acts: bfloat16 [2, 8192, 128], P(None, ('parts', 'width')), may hold values from 0.099609375 to 4
- enc_cols: bfloat16 [2, 1024, 4608], P('layer', None, 'width'), may hold values from -0.09375 to 0.09375
- dec_rows: bfloat16 [2, 2, 1024, 4608], P('layer', None, None, 'width'), may hold values from -6 to 6
Outputs:
- edges: float32 [2, 2, 1024, 1024], P(('parts', 'layer'), None, 'width')
The draws below stay inside these ranges and needn't reach their ends.
Inputs may be any that keep to these rules, and one draw needn't show every extreme that they name: `src_ids`: each token's 64 slots are distinct. `tgt_ids`: each token's 64 slots are distinct.
All inputs are finite; a program needn't handle non-finite values.
Results may differ from the reference program's by a relative error of at most 0.0003.
Values may be sent and summed in bfloat16 or wider, within the bound.
A program may use at most 128 MiB of HBM per device.

```python
import math
import jax
import jax.numpy as jnp
from jax import lax

D = 4608
K = 64
ACT = 1024
TOKENS = 16384


def draw_lists(key):
    segment = ACT // K
    subkeys = jax.random.split(key, 12)
    tokens = jnp.arange(TOKENS, dtype=jnp.int32)[:, None]
    first_slots = tokens % segment
    offsets = jnp.arange(K, dtype=jnp.int32)[None, :] * segment

    def skewed(first_key, second_key):
        first_draw = jax.random.randint(first_key, (TOKENS, K), 0, segment, dtype=jnp.int32)
        second_draw = jax.random.randint(second_key, (TOKENS, K), 0, segment, dtype=jnp.int32)
        return jnp.where(tokens < segment, first_slots, jnp.minimum(first_draw, second_draw))
    source_raw = [skewed(subkeys[0], subkeys[1]), skewed(subkeys[2], subkeys[3])]
    target_raw = []
    for u in range(2):
        fresh_raw = jax.random.randint(subkeys[4 + u], (TOKENS, K), 0, segment, dtype=jnp.int32)
        source_pick = jax.random.randint(subkeys[6 + u], (TOKENS, K), 0, 3, dtype=jnp.int32)
        mixed_raw = jnp.where(source_pick == 0, source_raw[0], jnp.where(source_pick == 1, source_raw[1], fresh_raw))
        target_raw.append(jnp.where(tokens < segment, first_slots, mixed_raw))

    def labelled(raw_slots, label_key):
        labels_map = jax.random.permutation(label_key, ACT).astype(jnp.int32)
        return labels_map[offsets + raw_slots].reshape(TOKENS // 2, 2 * K)
    sources = jnp.stack([labelled(source_raw[s], subkeys[8 + s]) for s in range(2)])
    targets = jnp.stack([labelled(target_raw[u], subkeys[10 + u]) for u in range(2)])
    return (sources, targets)


def draw_src_ids(key, part):
    return draw_lists(key)[0]


def draw_tgt_ids(key, part):
    return draw_lists(key)[1]


def block_levels(key, extent, shards, low, high):
    def one(dim, blocks):
        heights = jax.random.uniform(jax.random.fold_in(jax.random.fold_in(key, 6), dim), (blocks,), jnp.float32, low / len(shards), high / len(shards))
        return jnp.repeat(jnp.exp(heights), extent[dim] // blocks).reshape((-1,) + (1,) * (len(extent) - dim - 1))

    level = one(*shards[0])
    for cut in shards[1:]:
        level = level * one(*cut)
    return level


def noise(key, shape, scale, bound, cuts=(), kind=jnp.bfloat16):
    level = block_levels(key, shape, cuts, -0.22, 0.18) if cuts else 1.0
    values = jax.random.normal(key, shape, jnp.float32) * scale * level
    return jnp.minimum(jnp.maximum(values, -bound), bound).astype(kind)


def setup_inputs(seed: int = 0, part: int = 0) -> dict:
    keys = jax.random.split(jax.random.key(seed), 7)
    own_keys = jax.random.split(jax.random.fold_in(keys[6], part), 7)
    src_ids = draw_src_ids(jax.random.fold_in(jax.random.fold_in(keys[6], part), 71), part)
    src_acts = jnp.clip(jnp.exp(math.log(4.0) - 3.6927934 * jax.random.uniform(own_keys[1], (2, TOKENS // 2, 2 * K), jnp.float32) ** block_levels(own_keys[1], (2, TOKENS // 2, 2 * K), ((0, 2), (1, 16)), -0.2, 0.2)), 0.099609375, 4.0).astype(jnp.bfloat16)
    tgt_ids = draw_tgt_ids(jax.random.fold_in(jax.random.fold_in(keys[6], part), 71), part)
    tgt_acts = jnp.clip(jnp.exp(math.log(4.0) - 3.6927934 * jax.random.uniform(own_keys[3], (2, TOKENS // 2, 2 * K), jnp.float32) ** block_levels(own_keys[3], (2, TOKENS // 2, 2 * K), ((1, 16),), -0.2, 0.2)), 0.099609375, 4.0).astype(jnp.bfloat16)
    enc_cols = noise(keys[4], (2, ACT, D), D ** -0.5, 0.09375, ((0, 2), (2, 16)))
    dec_rows = noise(keys[5], (2, 2, ACT, D), 1.0, 6.0, ((0, 2), (3, 16)))
    return {"src_ids": src_ids, "src_acts": src_acts, "tgt_ids": tgt_ids, "tgt_acts": tgt_acts, "enc_cols": enc_cols, "dec_rows": dec_rows}


def dense_acts(ids, acts):
    flat_ids = ids.reshape(ids.shape[0] * 2, ids.shape[1] // 2)
    flat_acts = acts.reshape(acts.shape[0] * 2, acts.shape[1] // 2)
    rows = jnp.arange(flat_ids.shape[0], dtype=jnp.int32)[:, None]
    return jnp.zeros((flat_ids.shape[0], ACT), jnp.bfloat16).at[rows, flat_ids].set(flat_acts.astype(jnp.bfloat16))


def reference(src_ids, src_acts, tgt_ids, tgt_acts, enc_cols, dec_rows):
    factor = (ACT / K) ** 2 / TOKENS
    targets = [dense_acts(tgt_ids[u], tgt_acts[u]) for u in range(2)]
    result = []
    for s in range(2):
        source = dense_acts(src_ids[s], src_acts[s])
        row_out = []
        for u in range(2):
            virt = lax.dot_general(dec_rows[s, u], enc_cols[u], (((1,), (1,)), ((), ())), preferred_element_type=jnp.float32)
            co_sum = lax.dot_general(source, targets[u], (((0,), (0,)), ((), ())), preferred_element_type=jnp.float32)
            row_out.append(virt * (co_sum * factor))
        result.append(jnp.stack(row_out))
    return jnp.stack(result)
```

```python
import functools

import jax
import jax.numpy as jnp
from jax import lax
from jax.experimental import pallas as pl
from jax.experimental.pallas import tpu as pltpu
from jax.sharding import PartitionSpec as P

MESH = pl.DeviceIdType.MESH
F32 = jnp.float32
BF16 = jnp.bfloat16
QUAD = 4
LANES = 128
UNROLL = 16


def build_dense(ids_ref, acts_ref, lo_s, key_s, act_s, tmp, put, high):
    rows, wide = ids_ref.shape
    per = QUAD * high
    ids = ids_ref[...].astype(jnp.int32)
    token = lax.broadcasted_iota(jnp.int32, ids.shape, 1) // (wide // QUAD)
    lo_s[...] = (ids % LANES).astype(F32)
    key_s[...] = (token * high + ids // LANES).astype(F32)
    act_s[...] = acts_ref[...].astype(F32)
    sub = lax.broadcasted_iota(jnp.int32, (16, wide), 0).astype(F32)

    def one(r):
        def row(ref):
            return jnp.broadcast_to(ref[pl.ds(r, 1), :], (16, wide)).astype(BF16)

        lo, key, act = row(lo_s), row(key_s), row(act_s)
        zero = jnp.zeros((16, wide), BF16)
        ones = jnp.ones((16, wide), BF16)
        b = jnp.concatenate(
            [jnp.where(lo == (sub + 16 * i).astype(BF16), ones, zero) for i in range(LANES // 16)], 0
        )
        a = jnp.concatenate(
            [jnp.where(key == (sub + 16 * i).astype(BF16), act, zero) for i in range(per // 16)], 0
        )
        out = lax.dot_general(a, b, (((1,), (1,)), ((), ())), preferred_element_type=F32)
        tmp[pl.ds(pl.multiple_of(r * per, per), per), :] = out

    def many(g, carry):
        for i in range(UNROLL):
            one(g * UNROLL + i)
        return carry

    lax.fori_loop(0, rows // UNROLL, many, 0)
    for j in range(QUAD):
        for h in range(high):
            put(j, h, tmp[pl.ds(j * high + h, rows, stride=per), :])


def kernel(
    groups, factor,
    sid_ref, sact_ref, tid_ref, tact_ref, enc_ref, dec_ref,
    out_ref,
    tid_g, tact_g, enc_own, enc_far, dec_g, src_out, src_g, tgt_own, tgt_far,
    part, arrived, lo_s, key_s, act_s, tmp,
    tid_ss, tid_rs, tact_ss, tact_rs, enc_ss, enc_rs, dec_ss, dec_rs, src_ss, src_rs,
    fe_ss, fe_rs, ft_ss, ft_rs, z_ss, z_rs,
):
    layer = lax.axis_index("layer")
    width = lax.axis_index("width")
    group, place = width // QUAD, width % QUAD
    rows = tid_ref.shape[0]
    count = enc_ref.shape[1]
    high = count // LANES
    share = count // QUAD
    block = share // groups
    pair = {"layer": 1 - layer}

    def xor(k):
        low, up = place % 2, place // 2
        low = low + (k % 2) * (1 - 2 * low)
        up = up + (k // 2) * (1 - 2 * up)
        return up * 2 + low

    peers = [xor(k) for k in range(QUAD)]
    ids = [{"width": group * QUAD + peers[k]} for k in range(QUAD)]
    ring = [lax.rem(group + s, groups) for s in range(groups)]
    ring_ids = [{"width": ring[s] * QUAD + place} for s in range(groups)]

    def remote(src, dst, ss, rs, to):
        return pltpu.make_async_remote_copy(
            src_ref=src, dst_ref=dst, send_sem=ss, recv_sem=rs, device_id=to, device_id_type=MESH
        )

    barrier = pltpu.get_barrier_semaphore()
    others = ids[1:] + ring_ids[1:] + [pair]
    for to in others:
        pl.semaphore_signal(barrier, inc=1, device_id=to, device_id_type=MESH)
    pl.semaphore_wait(barrier, len(others))

    tids = [remote(tid_ref, tid_g.at[k - 1], tid_ss.at[k - 1], tid_rs.at[k - 1], ids[k]) for k in range(1, QUAD)]
    tacts = [remote(tact_ref, tact_g.at[k - 1], tact_ss.at[k - 1], tact_rs.at[k - 1], ids[k]) for k in range(1, QUAD)]
    decs = [remote(dec_ref.at[peers[k]], dec_g.at[k], dec_ss.at[k - 1], dec_rs.at[k - 1], ids[k]) for k in range(1, QUAD)]
    encs = [remote(enc_ref, enc_own.at[k], enc_ss.at[k - 1], enc_rs.at[k - 1], ids[k]) for k in range(1, QUAD)]
    srcs = [remote(src_out.at[peers[k]], src_g.at[k - 1], src_ss.at[k - 1], src_rs.at[k - 1], ids[k]) for k in range(1, QUAD)]
    far_encs = [remote(enc_ref if k == 0 else enc_own.at[k], enc_far.at[k], fe_ss.at[k], fe_rs.at[k], pair) for k in range(QUAD)]
    far_tgts = [remote(tgt_own.at[k], tgt_far.at[k], ft_ss.at[k], ft_rs.at[k], pair) for k in range(QUAD)]
    sums = [
        [
            remote(
                part.at[i, pl.ds(pl.multiple_of(ring[s] * block, block), block), :],
                arrived.at[s - 1, i], z_ss.at[i, s - 1], z_rs.at[i, s - 1], ring_ids[s],
            )
            for s in range(1, groups)
        ]
        for i in range(4)
    ]

    for copies in (encs, decs, tids, tacts):
        for copy in copies:
            copy.start()
    far_encs[0].start()

    def put_source(j, h, v):
        per = share // LANES
        src_out[h // per, (h % per) * LANES:(h % per + 1) * LANES, j * rows:(j + 1) * rows] = v.T.astype(BF16)

    build_dense(sid_ref, sact_ref, lo_s, key_s, act_s, tmp, put_source, high)
    for copy in srcs:
        copy.start()

    enc_own[0] = enc_ref[...]
    dec_g[0] = dec_ref[place]

    def put_target(k):
        def put(j, h, v):
            tgt_own[k, j * rows:(j + 1) * rows, h * LANES:(h + 1) * LANES] = v.astype(BF16)

        return put

    tile = 256

    def co_add(i, k, target):
        source = src_out[place] if k == 0 else src_g[k - 1]

        @pl.loop(0, count // tile)
        def _(n):
            at = pl.ds(pl.multiple_of(n * tile, tile), tile)
            term = jnp.dot(source, target[k, :, at], preferred_element_type=F32)
            if k == 0:
                part[i, :, at] = term
            else:
                part[i, :, at] += term

    def virt(i, encoder):
        depth = QUAD * enc_ref.shape[0]
        decoder = dec_g[:, i].reshape(depth, share)
        decoder = decoder.astype(F32).T.astype(BF16)

        @pl.loop(0, count // tile)
        def _(n):
            at = pl.ds(pl.multiple_of(n * tile, tile), tile)
            part[2 + i, :, at] = jnp.dot(
                decoder, encoder[:, :, at].reshape(depth, tile), preferred_element_type=F32
            )

    build_dense(tid_ref, tact_ref, lo_s, key_s, act_s, tmp, put_target(0), high)
    far_tgts[0].start()
    co_add(0, 0, tgt_own)

    for k in range(1, QUAD):
        encs[k - 1].wait_recv()
        far_encs[k].start()
    for copy in decs:
        copy.wait_recv()
    virt(0, enc_own)
    for copy in sums[2]:
        copy.start()
    for copy in far_encs:
        copy.wait_recv()
    virt(1, enc_far)
    for copy in sums[3]:
        copy.start()

    for k in range(1, QUAD):
        tids[k - 1].wait_recv()
        tacts[k - 1].wait_recv()
        build_dense(tid_g.at[k - 1], tact_g.at[k - 1], lo_s, key_s, act_s, tmp, put_target(k), high)
        far_tgts[k].start()
        srcs[k - 1].wait_recv()
        co_add(0, k, tgt_own)
    for copy in sums[0]:
        copy.start()
    for k in range(QUAD):
        far_tgts[k].wait_recv()
        co_add(1, k, tgt_far)
    for copy in sums[1]:
        copy.start()

    own = pl.ds(pl.multiple_of(group * block, block), block)

    def total(i):
        value = part[i, own, :]
        for s in range(1, groups):
            sums[i][s - 1].wait_recv()
            value = value + arrived[s - 1, i]
        return value

    for i, slot in ((0, layer), (1, 1 - layer)):
        out_ref[slot] = total(2 + i) * (total(i) * factor)

    for copies in (tids, tacts, decs, encs, srcs, far_encs, far_tgts, *sums):
        for copy in copies:
            copy.wait_send()


def on_device(src_ids, src_acts, tgt_ids, tgt_acts, enc_cols, dec_rows):
    layer = lax.axis_index("layer")
    shards = lax.axis_size("width")
    groups = shards // QUAD
    count, depth = enc_cols.shape[1:]
    share = count // QUAD
    block = share // groups
    top = src_ids.shape[2] // 2
    tokens = src_ids.shape[1] * 2
    rows, wide = tokens // QUAD, QUAD * top
    factor = (count / top) ** 2 / (tokens * shards)

    def pick(value, index):
        return lax.dynamic_index_in_dim(value, index, 0, False)

    ids = src_ids[0]
    ids = (ids // block % QUAD) * share + ids // (block * QUAD) * block + ids % block
    sid = ids.astype(jnp.int16).reshape(rows, wide)
    sact = src_acts[0].reshape(rows, wide)
    tid = pick(tgt_ids, layer).astype(jnp.int16).reshape(rows, wide)
    tact = pick(tgt_acts, layer).reshape(rows, wide)

    spare = -depth % 16
    enc = jnp.pad(enc_cols[0].T, ((0, spare), (0, 0)))
    dec = dec_rows[0]
    dec = jnp.where(layer == 0, dec, dec[::-1])
    dec = dec.reshape(2, groups, QUAD, block, depth).transpose(2, 0, 4, 1, 3)
    dec = jnp.pad(dec.reshape(QUAD, 2, depth, share), ((0, 0), (0, 0), (0, spare), (0, 0)))
    deep = depth + spare

    def vmem(*shape, kind=BF16):
        return pltpu.VMEM(shape, kind)

    def sems(*shape):
        return [pltpu.SemaphoreType.DMA(shape)] * 2

    out = pl.pallas_call(
        functools.partial(kernel, groups, factor),
        out_shape=jax.ShapeDtypeStruct((2, block, count), F32),
        in_specs=[pl.BlockSpec(memory_space=pltpu.VMEM)] * 6,
        out_specs=pl.BlockSpec(memory_space=pltpu.VMEM),
        scratch_shapes=[
            vmem(QUAD - 1, rows, wide, kind=jnp.int16),
            vmem(QUAD - 1, rows, wide),
            vmem(QUAD, deep, count),
            vmem(QUAD, deep, count),
            vmem(QUAD, 2, deep, share),
            vmem(QUAD, share, tokens),
            vmem(QUAD - 1, share, tokens),
            vmem(QUAD, tokens, count),
            vmem(QUAD, tokens, count),
            vmem(4, share, count, kind=F32),
            vmem(groups - 1, 4, block, count, kind=F32),
            vmem(rows, wide, kind=F32),
            vmem(rows, wide, kind=F32),
            vmem(rows, wide, kind=F32),
            vmem(rows * QUAD * (count // LANES), LANES, kind=F32),
            *sems(QUAD - 1),
            *sems(QUAD - 1),
            *sems(QUAD - 1),
            *sems(QUAD - 1),
            *sems(QUAD - 1),
            *sems(QUAD),
            *sems(QUAD),
            *sems(4, groups - 1),
        ],
        compiler_params=pltpu.CompilerParams(
            collective_id=0, has_side_effects=True, vmem_limit_bytes=56 * 1024 * 1024
        ),
        name="edges",
    )(sid, sact, tid, tact, enc, dec)
    return out[None]


def solution(mesh):
    placed = (
        P("layer", ("parts", "width"), None),
        P("layer", ("parts", "width"), None),
        P(None, ("parts", "width"), None),
        P(None, ("parts", "width"), None),
        P("layer", None, "width"),
        P("layer", None, None, "width"),
    )
    return jax.shard_map(
        on_device,
        mesh=mesh,
        in_specs=placed,
        out_specs=P(("parts", "layer"), None, "width", None),
        check_vma=False,
    )
```

```python
import functools

import jax
import jax.numpy as jnp
from jax import lax
from jax.experimental import pallas as pl
from jax.experimental.pallas import tpu as pltpu
from jax.sharding import PartitionSpec as P

MESH = pl.DeviceIdType.MESH
F32 = jnp.float32
BF16 = jnp.bfloat16
QUAD = 4
LANES = 128
UNROLL = 16
TILE = 256
LEVELS = 32766.0


def build_dense(ids_ref, acts_ref, lo_s, key_s, act_s, tmp, put, high):
    rows, wide = ids_ref.shape
    per = QUAD * high
    ids = ids_ref[...].astype(jnp.int32)
    token = lax.broadcasted_iota(jnp.int32, ids.shape, 1) // (wide // QUAD)
    lo_s[...] = (ids % LANES).astype(F32)
    key_s[...] = (token * high + ids // LANES).astype(F32)
    act_s[...] = acts_ref[...].astype(F32)
    sub = lax.broadcasted_iota(jnp.int32, (16, wide), 0).astype(F32)

    def one(r):
        def row(ref):
            return jnp.broadcast_to(ref[pl.ds(r, 1), :], (16, wide)).astype(BF16)

        lo, key, act = row(lo_s), row(key_s), row(act_s)
        zero = jnp.zeros((16, wide), BF16)
        ones = jnp.ones((16, wide), BF16)
        b = jnp.concatenate(
            [jnp.where(lo == (sub + 16 * i).astype(BF16), ones, zero) for i in range(LANES // 16)], 0
        )
        a = jnp.concatenate(
            [jnp.where(key == (sub + 16 * i).astype(BF16), act, zero) for i in range(per // 16)], 0
        )
        out = lax.dot_general(a, b, (((1,), (1,)), ((), ())), preferred_element_type=F32)
        tmp[pl.ds(pl.multiple_of(r * per, per), per), :] = out

    def many(g, carry):
        for i in range(UNROLL):
            one(g * UNROLL + i)
        return carry

    lax.fori_loop(0, rows // UNROLL, many, 0)
    for j in range(QUAD):
        for h in range(high):
            put(j, h, tmp[pl.ds(j * high + h, rows, stride=per), :])


def kernel(
    groups, factor,
    sid_ref, sact_ref, tid_ref, tact_ref, enc_ref, dec_ref,
    out_ref,
    tid_g, tact_g, enc_own, enc_far, dec_g, src_out, src_g, tgt_own, tgt_far,
    part, code, scale, code_in, scale_in, dec_t, lo_s, key_s, act_s, tmp,
    tid_ss, tid_rs, tact_ss, tact_rs, enc_ss, enc_rs, dec_ss, dec_rs, src_ss, src_rs,
    fe_ss, fe_rs, ft_ss, ft_rs, code_ss, code_rs, scale_ss, scale_rs,
):
    layer = lax.axis_index("layer")
    width = lax.axis_index("width")
    group, place = width // QUAD, width % QUAD
    rows = tid_ref.shape[0]
    tiles = enc_ref.shape[0]
    count = tiles * TILE
    high = count // LANES
    share = count // QUAD
    block = share // groups
    pair = {"layer": 1 - layer}

    def xor(k):
        low, up = place % 2, place // 2
        low = low + (k % 2) * (1 - 2 * low)
        up = up + (k // 2) * (1 - 2 * up)
        return up * 2 + low

    peers = [xor(k) for k in range(QUAD)]
    ids = [{"width": group * QUAD + peers[k]} for k in range(QUAD)]
    ring = [lax.rem(group + s, groups) for s in range(groups)]
    ring_ids = [{"width": ring[s] * QUAD + place} for s in range(groups)]

    def remote(src, dst, ss, rs, to):
        return pltpu.make_async_remote_copy(
            src_ref=src, dst_ref=dst, send_sem=ss, recv_sem=rs, device_id=to, device_id_type=MESH
        )

    barrier = pltpu.get_barrier_semaphore()
    others = ids[1:] + ring_ids[1:] + [pair]
    for to in others:
        pl.semaphore_signal(barrier, inc=1, device_id=to, device_id_type=MESH)
    pl.semaphore_wait(barrier, len(others))

    tids = [remote(tid_ref, tid_g.at[k - 1], tid_ss.at[k - 1], tid_rs.at[k - 1], ids[k]) for k in range(1, QUAD)]
    tacts = [remote(tact_ref, tact_g.at[k - 1], tact_ss.at[k - 1], tact_rs.at[k - 1], ids[k]) for k in range(1, QUAD)]
    decs = [remote(dec_ref.at[peers[k]], dec_g.at[k], dec_ss.at[k - 1], dec_rs.at[k - 1], ids[k]) for k in range(1, QUAD)]
    encs = [
        [remote(enc_ref.at[n], enc_own.at[n, k], enc_ss.at[n, k - 1], enc_rs.at[n, k - 1], ids[k]) for k in range(1, QUAD)]
        for n in range(tiles)
    ]
    srcs = [remote(src_out.at[peers[k]], src_g.at[k - 1], src_ss.at[k - 1], src_rs.at[k - 1], ids[k]) for k in range(1, QUAD)]
    far_encs = [remote(enc_own.at[n], enc_far.at[n], fe_ss.at[n], fe_rs.at[n], pair) for n in range(tiles)]
    far_tgts = [remote(tgt_own.at[k], tgt_far.at[k], ft_ss.at[k], ft_rs.at[k], pair) for k in range(QUAD)]
    stages = [(slice(0, 1), slice(None)), (slice(1, 2), slice(None))]
    stages += [(slice(2, 4), slice(n, n + 1)) for n in range(tiles)]

    def stage_copies(c, s):
        i, n = stages[c]
        rows_to = pl.ds(pl.multiple_of(ring[s] * block, block), block)
        return (
            remote(code.at[i, n, rows_to, :], code_in.at[s - 1, i, n], code_ss.at[c, s - 1], code_rs.at[c, s - 1], ring_ids[s]),
            remote(scale.at[ring[s], i, n], scale_in.at[s - 1, i, n], scale_ss.at[c, s - 1], scale_rs.at[c, s - 1], ring_ids[s]),
        )

    sums = [[copy for s in range(1, groups) for copy in stage_copies(c, s)] for c in range(len(stages))]

    for copies in (tids, tacts):
        for copy in copies:
            copy.start()

    def encode(i, n):
        for g in range(groups):
            at = pl.ds(g * block, block)
            value = part[i, n, at, :]
            size = jnp.abs(value)
            top = jnp.max(size, axis=0, keepdims=True)
            inverse = jnp.where(top > 0, 1.0 / top, 0.0)
            level = (jnp.sqrt(size * inverse) * LEVELS + 0.5).astype(jnp.int32)
            code[i, n, at, :] = jnp.where(value < 0, -level, level).astype(jnp.int16)
            scale[g, i, n] = top * (1.0 / LEVELS**2)

    def put_source(j, h, v):
        per = share // LANES
        src_out[h // per, (h % per) * LANES:(h % per + 1) * LANES, j * rows:(j + 1) * rows] = v.T.astype(BF16)

    build_dense(sid_ref, sact_ref, lo_s, key_s, act_s, tmp, put_source, high)
    for copy in srcs + decs:
        copy.start()

    enc_own[:, 0] = enc_ref[...]
    dec_g[0] = dec_ref[place]

    def put_target(k):
        def put(j, h, v):
            tgt_own[k, j * rows:(j + 1) * rows, h * LANES:(h + 1) * LANES] = v.astype(BF16)

        return put

    def co_add(i, k, target):
        source = src_out[place] if k == 0 else src_g[k - 1]

        @pl.loop(0, tiles)
        def _(n):
            at = pl.ds(pl.multiple_of(n * TILE, TILE), TILE)
            term = jnp.dot(source, target[k, :, at], preferred_element_type=F32)
            if k == 0:
                part[i, n] = term
            else:
                part[i, n] += term
            if k == QUAD - 1:
                encode(i, n)

    depth = QUAD * enc_ref.shape[1]

    def virt(i, n, encoder):
        part[2 + i, n] = jnp.dot(
            dec_t[i], encoder[n].reshape(depth, TILE), preferred_element_type=F32
        )
        encode(2 + i, n)

    build_dense(tid_ref, tact_ref, lo_s, key_s, act_s, tmp, put_target(0), high)
    far_tgts[0].start()
    co_add(0, 0, tgt_own)

    for copies in encs:
        for copy in copies:
            copy.start()

    for k in range(1, QUAD):
        tids[k - 1].wait_recv()
        tacts[k - 1].wait_recv()
        build_dense(tid_g.at[k - 1], tact_g.at[k - 1], lo_s, key_s, act_s, tmp, put_target(k), high)
        far_tgts[k].start()
        srcs[k - 1].wait_recv()
        co_add(0, k, tgt_own)
    for copy in sums[0]:
        copy.start()
    for k in range(QUAD):
        far_tgts[k].wait_recv()
        co_add(1, k, tgt_far)
    for copy in sums[1]:
        copy.start()

    for copy in decs:
        copy.wait_recv()
    for i in range(2):
        dec_t[i] = dec_g[:, i].reshape(depth, share).astype(F32).T.astype(BF16)
    for n in range(tiles):
        for copy in encs[n]:
            copy.wait_recv()
        far_encs[n].start()
        virt(0, n, enc_own)
        far_encs[n].wait_recv()
        virt(1, n, enc_far)
        for copy in sums[2 + n]:
            copy.start()

    own = pl.ds(pl.multiple_of(group * block, block), block)

    def total(i, n):
        value = part[i, n, own, :]
        for s in range(groups - 1):
            level = code_in[s, i, n].astype(jnp.int32).astype(F32)
            value = value + level * jnp.abs(level) * scale_in[s, i, n]
        return value

    for c in range(2):
        for copy in sums[c]:
            copy.wait_recv()
    for n in range(tiles):
        for copy in sums[2 + n]:
            copy.wait_recv()
        for i, slot in ((0, layer), (1, 1 - layer)):
            out_ref[slot, :, n * TILE:(n + 1) * TILE] = total(2 + i, n) * (total(i, n) * factor)

    for copies in (tids, tacts, decs, *encs, srcs, far_encs, far_tgts, *sums):
        for copy in copies:
            copy.wait_send()


def on_device(src_ids, src_acts, tgt_ids, tgt_acts, enc_cols, dec_rows):
    layer = lax.axis_index("layer")
    shards = lax.axis_size("width")
    groups = shards // QUAD
    count, depth = enc_cols.shape[1:]
    share = count // QUAD
    block = share // groups
    top = src_ids.shape[2] // 2
    tokens = src_ids.shape[1] * 2
    rows, wide = tokens // QUAD, QUAD * top
    factor = (count / top) ** 2 / (tokens * shards)

    def pick(value, index):
        return lax.dynamic_index_in_dim(value, index, 0, False)

    ids = src_ids[0]
    ids = (ids // block % QUAD) * share + ids // (block * QUAD) * block + ids % block
    sid = ids.astype(jnp.int16).reshape(rows, wide)
    sact = src_acts[0].reshape(rows, wide)
    tid = pick(tgt_ids, layer).astype(jnp.int16).reshape(rows, wide)
    tact = pick(tgt_acts, layer).reshape(rows, wide)

    spare = -depth % 16
    enc = jnp.pad(enc_cols[0].T, ((0, spare), (0, 0)))
    dec = dec_rows[0]
    dec = jnp.where(layer == 0, dec, dec[::-1])
    dec = dec.reshape(2, groups, QUAD, block, depth).transpose(2, 0, 4, 1, 3)
    dec = jnp.pad(dec.reshape(QUAD, 2, depth, share), ((0, 0), (0, 0), (0, spare), (0, 0)))
    deep = depth + spare
    tiles = count // TILE
    enc = enc.reshape(deep, tiles, TILE).transpose(1, 0, 2)

    def vmem(*shape, kind=BF16):
        return pltpu.VMEM(shape, kind)

    def sems(*shape):
        return [pltpu.SemaphoreType.DMA(shape)] * 2

    out = pl.pallas_call(
        functools.partial(kernel, groups, factor),
        out_shape=jax.ShapeDtypeStruct((2, block, count), F32),
        in_specs=[pl.BlockSpec(memory_space=pltpu.VMEM)] * 6,
        out_specs=pl.BlockSpec(memory_space=pltpu.VMEM),
        scratch_shapes=[
            vmem(QUAD - 1, rows, wide, kind=jnp.int16),
            vmem(QUAD - 1, rows, wide),
            vmem(tiles, QUAD, deep, TILE),
            vmem(tiles, QUAD, deep, TILE),
            vmem(QUAD, 2, deep, share),
            vmem(QUAD, share, tokens),
            vmem(QUAD - 1, share, tokens),
            vmem(QUAD, tokens, count),
            vmem(QUAD, tokens, count),
            vmem(4, tiles, share, TILE, kind=F32),
            vmem(4, tiles, share, TILE, kind=jnp.int16),
            vmem(groups, 4, tiles, 1, TILE, kind=F32),
            vmem(groups - 1, 4, tiles, block, TILE, kind=jnp.int16),
            vmem(groups - 1, 4, tiles, 1, TILE, kind=F32),
            vmem(2, share, QUAD * deep),
            vmem(rows, wide, kind=F32),
            vmem(rows, wide, kind=F32),
            vmem(rows, wide, kind=F32),
            vmem(rows * QUAD * (count // LANES), LANES, kind=F32),
            *sems(QUAD - 1),
            *sems(QUAD - 1),
            *sems(tiles, QUAD - 1),
            *sems(QUAD - 1),
            *sems(QUAD - 1),
            *sems(tiles),
            *sems(QUAD),
            *sems(2 + tiles, groups - 1),
            *sems(2 + tiles, groups - 1),
        ],
        compiler_params=pltpu.CompilerParams(
            collective_id=0, has_side_effects=True, vmem_limit_bytes=56 * 1024 * 1024
        ),
        name="edges",
    )(sid, sact, tid, tact, enc, dec)
    return out[None]


def solution(mesh):
    placed = (
        P("layer", ("parts", "width"), None),
        P("layer", ("parts", "width"), None),
        P(None, ("parts", "width"), None),
        P(None, ("parts", "width"), None),
        P("layer", None, "width"),
        P("layer", None, None, "width"),
    )
    return jax.shard_map(
        on_device,
        mesh=mesh,
        in_specs=placed,
        out_specs=P(("parts", "layer"), None, "width", None),
        check_vma=False,
    )
```

```python
import functools

import jax
import jax.numpy as jnp
from jax import lax
from jax.experimental import pallas as pl
from jax.experimental.pallas import tpu as pltpu
from jax.sharding import PartitionSpec as P

MESH = pl.DeviceIdType.MESH
F32 = jnp.float32
BF16 = jnp.bfloat16
QUAD = 4
LANES = 128
UNROLL = 32
TILE = 256
LEVELS = 32766.0


def build_dense(ids_ref, acts_ref, lo_s, key_s, act_s, tmp, put, high):
    rows, wide = ids_ref.shape
    per = QUAD * high
    step = per + 8
    ids = ids_ref[...].astype(jnp.int32)
    token = lax.broadcasted_iota(jnp.int32, ids.shape, 1) // (wide // QUAD)
    lo_s[...] = (ids % LANES).astype(F32)
    key_s[...] = (token * high + ids // LANES).astype(F32)
    act_s[...] = acts_ref[...].astype(F32)
    sub = lax.broadcasted_iota(jnp.int32, (16, wide), 0).astype(F32)

    def one(r):
        def row(ref):
            return jnp.broadcast_to(ref[pl.ds(r, 1), :], (16, wide)).astype(BF16)

        lo, key, act = row(lo_s), row(key_s), row(act_s)
        zero = jnp.zeros((16, wide), BF16)
        ones = jnp.ones((16, wide), BF16)
        b = jnp.concatenate(
            [jnp.where(lo == (sub + 16 * i).astype(BF16), ones, zero) for i in range(LANES // 16)], 0
        )
        a = jnp.concatenate(
            [jnp.where(key == (sub + 16 * i).astype(BF16), act, zero) for i in range(per // 16)], 0
        )
        out = lax.dot_general(a, b, (((1,), (1,)), ((), ())), preferred_element_type=F32)
        tmp[pl.ds(pl.multiple_of(r * step, 8), per), :] = out

    def many(g, carry):
        for i in range(UNROLL):
            one(g * UNROLL + i)
        return carry

    lax.fori_loop(0, rows // UNROLL, many, 0)
    for j in range(QUAD):
        for h in range(high):
            put(j, h, tmp[pl.ds(j * high + h, rows, stride=step), :])


def kernel(
    groups, factor,
    sid_ref, sact_ref, tid_ref, tact_ref, enc_ref, dec_ref,
    out_ref,
    tid_g, tact_g, enc_own, enc_far, dec_g, src_out, src_g, tgt_own, tgt_far,
    part, code, scale, code_in, scale_in, dec_t, lo_s, key_s, act_s, tmp,
    tid_ss, tid_rs, tact_ss, tact_rs, enc_ss, enc_rs, dec_ss, dec_rs, src_ss, src_rs,
    fe_ss, fe_rs, ft_ss, ft_rs, code_ss, code_rs, scale_ss, scale_rs,
):
    layer = lax.axis_index("layer")
    width = lax.axis_index("width")
    group, place = width // QUAD, width % QUAD
    rows = tid_ref.shape[0]
    tiles = enc_ref.shape[0]
    count = tiles * TILE
    high = count // LANES
    share = count // QUAD
    block = share // groups
    pair = {"layer": 1 - layer}

    def xor(k):
        low, up = place % 2, place // 2
        low = low + (k % 2) * (1 - 2 * low)
        up = up + (k // 2) * (1 - 2 * up)
        return up * 2 + low

    peers = [xor(k) for k in range(QUAD)]
    ids = [{"width": group * QUAD + peers[k]} for k in range(QUAD)]
    ring = [lax.rem(group + s, groups) for s in range(groups)]
    ring_ids = [{"width": ring[s] * QUAD + place} for s in range(groups)]

    def remote(src, dst, ss, rs, to):
        return pltpu.make_async_remote_copy(
            src_ref=src, dst_ref=dst, send_sem=ss, recv_sem=rs, device_id=to, device_id_type=MESH
        )

    barrier = pltpu.get_barrier_semaphore()
    others = ids[1:] + ring_ids[1:] + [pair]
    for to in others:
        pl.semaphore_signal(barrier, inc=1, device_id=to, device_id_type=MESH)
    pl.semaphore_wait(barrier, len(others))

    tids = [remote(tid_ref, tid_g.at[k - 1], tid_ss.at[k - 1], tid_rs.at[k - 1], ids[k]) for k in range(1, QUAD)]
    tacts = [remote(tact_ref, tact_g.at[k - 1], tact_ss.at[k - 1], tact_rs.at[k - 1], ids[k]) for k in range(1, QUAD)]
    decs = [remote(dec_ref.at[peers[k]], dec_g.at[k], dec_ss.at[k - 1], dec_rs.at[k - 1], ids[k]) for k in range(1, QUAD)]
    encs = [
        [remote(enc_ref.at[n], enc_own.at[n, k], enc_ss.at[n, k - 1], enc_rs.at[n, k - 1], ids[k]) for k in range(1, QUAD)]
        for n in range(tiles)
    ]
    srcs = [remote(src_out.at[peers[k]], src_g.at[k - 1], src_ss.at[k - 1], src_rs.at[k - 1], ids[k]) for k in range(1, QUAD)]
    far_encs = [remote(enc_own.at[n], enc_far.at[n], fe_ss.at[n], fe_rs.at[n], pair) for n in range(tiles)]
    far_tgts = [remote(tgt_own.at[k], tgt_far.at[k], ft_ss.at[k], ft_rs.at[k], pair) for k in range(QUAD)]
    stages = [(slice(0, 1), slice(None)), (slice(1, 2), slice(None))]
    stages += [(slice(2, 4), slice(n, n + 1)) for n in range(tiles)]

    def stage_copies(c, s):
        i, n = stages[c]
        rows_to = pl.ds(pl.multiple_of(ring[s] * block, block), block)
        return (
            remote(code.at[i, n, rows_to, :], code_in.at[s - 1, i, n], code_ss.at[c, s - 1], code_rs.at[c, s - 1], ring_ids[s]),
            remote(scale.at[ring[s], i, n], scale_in.at[s - 1, i, n], scale_ss.at[c, s - 1], scale_rs.at[c, s - 1], ring_ids[s]),
        )

    sums = [[copy for s in range(1, groups) for copy in stage_copies(c, s)] for c in range(len(stages))]

    for copies in (tids, tacts, decs, *encs):
        for copy in copies:
            copy.start()

    def encode(i, n):
        for g in range(groups):
            at = pl.ds(g * block, block)
            value = part[i, n, at, :]
            size = jnp.abs(value)
            top = jnp.max(size, axis=0, keepdims=True)
            inverse = jnp.where(top > 0, 1.0 / top, 0.0)
            level = (jnp.sqrt(size * inverse) * LEVELS + 0.5).astype(jnp.int32)
            code[i, n, at, :] = jnp.where(value < 0, -level, level).astype(jnp.int16)
            scale[g, i, n] = top * (1.0 / LEVELS**2)

    def put_source(j, h, v):
        per = share // LANES
        src_out[h // per, (h % per) * LANES:(h % per + 1) * LANES, j * rows:(j + 1) * rows] = v.T.astype(BF16)

    build_dense(sid_ref, sact_ref, lo_s, key_s, act_s, tmp, put_source, high)
    for copy in srcs:
        copy.start()

    enc_own[:, 0] = enc_ref[...]
    dec_g[0] = dec_ref[place]

    def put_target(k):
        def put(j, h, v):
            tgt_own[k, j * rows:(j + 1) * rows, h * LANES:(h + 1) * LANES] = v.astype(BF16)

        return put

    def co_add(i, k, target):
        source = src_out[place] if k == 0 else src_g[k - 1]

        @pl.loop(0, tiles)
        def _(n):
            at = pl.ds(pl.multiple_of(n * TILE, TILE), TILE)
            term = jnp.dot(source, target[k, :, at], preferred_element_type=F32)
            if k == 0:
                part[i, n] = term
            else:
                part[i, n] += term
            if k == QUAD - 1:
                encode(i, n)

    depth = QUAD * enc_ref.shape[1]

    def virt(i, n, encoder):
        part[2 + i, n] = jnp.dot(
            dec_t[i], encoder[n].reshape(depth, TILE), preferred_element_type=F32
        )
        encode(2 + i, n)

    build_dense(tid_ref, tact_ref, lo_s, key_s, act_s, tmp, put_target(0), high)
    far_tgts[0].start()
    co_add(0, 0, tgt_own)

    def target_of(k):
        tids[k - 1].wait_recv()
        tacts[k - 1].wait_recv()
        build_dense(tid_g.at[k - 1], tact_g.at[k - 1], lo_s, key_s, act_s, tmp, put_target(k), high)
        far_tgts[k].start()

    target_of(1)
    target_of(2)
    for copy in decs:
        copy.wait_recv()
    for i in range(2):
        dec_t[i] = dec_g[:, i].reshape(depth, share).astype(F32).T.astype(BF16)
    for n in range(tiles):
        for copy in encs[n]:
            copy.wait_recv()
        far_encs[n].start()
        virt(0, n, enc_own)
        far_encs[n].wait_recv()
        virt(1, n, enc_far)
        for copy in sums[2 + n]:
            copy.start()

    target_of(3)
    for k in range(1, QUAD):
        srcs[k - 1].wait_recv()
        co_add(0, k, tgt_own)
    for copy in sums[0]:
        copy.start()
    for k in range(QUAD):
        far_tgts[k].wait_recv()
        co_add(1, k, tgt_far)
    for copy in sums[1]:
        copy.start()

    own = pl.ds(pl.multiple_of(group * block, block), block)

    def total(i, n):
        value = part[i, n, own, :]
        for s in range(groups - 1):
            level = code_in[s, i, n].astype(jnp.int32).astype(F32)
            value = value + level * jnp.abs(level) * scale_in[s, i, n]
        return value

    for c in range(2):
        for copy in sums[c]:
            copy.wait_recv()
    for n in range(tiles):
        for copy in sums[2 + n]:
            copy.wait_recv()
        for i, slot in ((0, layer), (1, 1 - layer)):
            out_ref[slot, :, n * TILE:(n + 1) * TILE] = total(2 + i, n) * (total(i, n) * factor)

    for copies in (tids, tacts, decs, *encs, srcs, far_encs, far_tgts, *sums):
        for copy in copies:
            copy.wait_send()


def on_device(src_ids, src_acts, tgt_ids, tgt_acts, enc_cols, dec_rows):
    layer = lax.axis_index("layer")
    shards = lax.axis_size("width")
    groups = shards // QUAD
    count, depth = enc_cols.shape[1:]
    share = count // QUAD
    block = share // groups
    top = src_ids.shape[2] // 2
    tokens = src_ids.shape[1] * 2
    rows, wide = tokens // QUAD, QUAD * top
    factor = (count / top) ** 2 / (tokens * shards)

    def pick(value, index):
        return lax.dynamic_index_in_dim(value, index, 0, False)

    ids = src_ids[0]
    ids = (ids // block % QUAD) * share + ids // (block * QUAD) * block + ids % block
    sid = ids.astype(jnp.int16).reshape(rows, wide)
    sact = src_acts[0].reshape(rows, wide)
    tid = pick(tgt_ids, layer).astype(jnp.int16).reshape(rows, wide)
    tact = pick(tgt_acts, layer).reshape(rows, wide)

    spare = -depth % 16
    enc = jnp.pad(enc_cols[0].T, ((0, spare), (0, 0)))
    dec = dec_rows[0]
    dec = jnp.where(layer == 0, dec, dec[::-1])
    dec = dec.reshape(2, groups, QUAD, block, depth).transpose(2, 0, 4, 1, 3)
    dec = jnp.pad(dec.reshape(QUAD, 2, depth, share), ((0, 0), (0, 0), (0, spare), (0, 0)))
    deep = depth + spare
    tiles = count // TILE
    enc = enc.reshape(deep, tiles, TILE).transpose(1, 0, 2)

    def vmem(*shape, kind=BF16):
        return pltpu.VMEM(shape, kind)

    def sems(*shape):
        return [pltpu.SemaphoreType.DMA(shape)] * 2

    out = pl.pallas_call(
        functools.partial(kernel, groups, factor),
        out_shape=jax.ShapeDtypeStruct((2, block, count), F32),
        in_specs=[pl.BlockSpec(memory_space=pltpu.VMEM)] * 6,
        out_specs=pl.BlockSpec(memory_space=pltpu.VMEM),
        scratch_shapes=[
            vmem(QUAD - 1, rows, wide, kind=jnp.int16),
            vmem(QUAD - 1, rows, wide),
            vmem(tiles, QUAD, deep, TILE),
            vmem(tiles, QUAD, deep, TILE),
            vmem(QUAD, 2, deep, share),
            vmem(QUAD, share, tokens),
            vmem(QUAD - 1, share, tokens),
            vmem(QUAD, tokens, count),
            vmem(QUAD, tokens, count),
            vmem(4, tiles, share, TILE, kind=F32),
            vmem(4, tiles, share, TILE, kind=jnp.int16),
            vmem(groups, 4, tiles, 1, TILE, kind=F32),
            vmem(groups - 1, 4, tiles, block, TILE, kind=jnp.int16),
            vmem(groups - 1, 4, tiles, 1, TILE, kind=F32),
            vmem(2, share, QUAD * deep),
            vmem(rows, wide, kind=F32),
            vmem(rows, wide, kind=F32),
            vmem(rows, wide, kind=F32),
            vmem(rows * (QUAD * (count // LANES) + 8), LANES, kind=F32),
            *sems(QUAD - 1),
            *sems(QUAD - 1),
            *sems(tiles, QUAD - 1),
            *sems(QUAD - 1),
            *sems(QUAD - 1),
            *sems(tiles),
            *sems(QUAD),
            *sems(2 + tiles, groups - 1),
            *sems(2 + tiles, groups - 1),
        ],
        compiler_params=pltpu.CompilerParams(
            collective_id=0, has_side_effects=True, vmem_limit_bytes=56 * 1024 * 1024
        ),
        name="edges",
    )(sid, sact, tid, tact, enc, dec)
    return out[None]


def solution(mesh):
    placed = (
        P("layer", ("parts", "width"), None),
        P("layer", ("parts", "width"), None),
        P(None, ("parts", "width"), None),
        P(None, ("parts", "width"), None),
        P("layer", None, "width"),
        P("layer", None, None, "width"),
    )
    return jax.shard_map(
        on_device,
        mesh=mesh,
        in_specs=placed,
        out_specs=P(("parts", "layer"), None, "width", None),
        check_vma=False,
    )
```

```python
import functools

import jax
import jax.numpy as jnp
from jax import lax
from jax.experimental import pallas as pl
from jax.experimental.pallas import tpu as pltpu
from jax.sharding import PartitionSpec as P

MESH = pl.DeviceIdType.MESH
F32 = jnp.float32
BF16 = jnp.bfloat16
QUAD = 4
LANES = 128
UNROLL = 32
TILE = 256
LEVELS = 32766.0


def build_dense(ids_ref, acts_ref, lo_s, key_s, act_s, tmp, put, high):
    rows, wide = ids_ref.shape
    per = QUAD * high
    step = per + 8
    ids = ids_ref[...].astype(jnp.int32)
    token = lax.broadcasted_iota(jnp.int32, ids.shape, 1) // (wide // QUAD)
    lo_s[...] = (ids % LANES).astype(F32)
    key_s[...] = (token * high + ids // LANES).astype(F32)
    act_s[...] = acts_ref[...].astype(F32)
    sub = lax.broadcasted_iota(jnp.int32, (16, wide), 0).astype(F32)

    def one(r):
        def row(ref):
            return jnp.broadcast_to(ref[pl.ds(r, 1), :], (16, wide)).astype(BF16)

        lo, key, act = row(lo_s), row(key_s), row(act_s)
        zero = jnp.zeros((16, wide), BF16)
        ones = jnp.ones((16, wide), BF16)
        b = jnp.concatenate(
            [jnp.where(lo == (sub + 16 * i).astype(BF16), ones, zero) for i in range(LANES // 16)], 0
        )
        a = jnp.concatenate(
            [jnp.where(key == (sub + 16 * i).astype(BF16), act, zero) for i in range(per // 16)], 0
        )
        out = lax.dot_general(a, b, (((1,), (1,)), ((), ())), preferred_element_type=F32)
        tmp[pl.ds(pl.multiple_of(r * step, 8), per), :] = out

    def many(g, carry):
        for i in range(UNROLL):
            one(g * UNROLL + i)
        return carry

    lax.fori_loop(0, rows // UNROLL, many, 0)
    for j in range(QUAD):
        for h in range(high):
            put(j, h, tmp[pl.ds(j * high + h, rows, stride=step), :])


def kernel(
    groups, factor,
    sid_ref, sact_ref, tid_ref, tact_ref, enc_ref, dec_ref,
    out_ref,
    tid_g, tact_g, enc_own, enc_far, dec_g, src_out, src_g, tgt_own, tgt_far,
    part, code, scale, code_in, scale_in, dec_t, lo_s, key_s, act_s, tmp,
    tid_ss, tid_rs, tact_ss, tact_rs, enc_ss, enc_rs, dec_ss, dec_rs, src_ss, src_rs,
    fe_ss, fe_rs, ft_ss, ft_rs, code_ss, code_rs, scale_ss, scale_rs,
):
    layer = lax.axis_index("layer")
    width = lax.axis_index("width")
    group, place = width // QUAD, width % QUAD
    rows = tid_ref.shape[0]
    tiles = enc_ref.shape[0]
    count = tiles * TILE
    high = count // LANES
    share = count // QUAD
    block = share // groups
    pair = {"layer": 1 - layer}

    def xor(k):
        low, up = place % 2, place // 2
        low = low + (k % 2) * (1 - 2 * low)
        up = up + (k // 2) * (1 - 2 * up)
        return up * 2 + low

    peers = [xor(k) for k in range(QUAD)]
    ids = [{"width": group * QUAD + peers[k]} for k in range(QUAD)]
    ring = [lax.rem(group + s, groups) for s in range(groups)]
    ring_ids = [{"width": ring[s] * QUAD + place} for s in range(groups)]

    def remote(src, dst, ss, rs, to):
        return pltpu.make_async_remote_copy(
            src_ref=src, dst_ref=dst, send_sem=ss, recv_sem=rs, device_id=to, device_id_type=MESH
        )

    barrier = pltpu.get_barrier_semaphore()
    others = ids[1:] + ring_ids[1:] + [pair]
    for to in others:
        pl.semaphore_signal(barrier, inc=1, device_id=to, device_id_type=MESH)
    pl.semaphore_wait(barrier, len(others))

    tids = [remote(tid_ref, tid_g.at[k - 1], tid_ss.at[k - 1], tid_rs.at[k - 1], ids[k]) for k in range(1, QUAD)]
    tacts = [remote(tact_ref, tact_g.at[k - 1], tact_ss.at[k - 1], tact_rs.at[k - 1], ids[k]) for k in range(1, QUAD)]
    decs = [remote(dec_ref.at[peers[k]], dec_g.at[k], dec_ss.at[k - 1], dec_rs.at[k - 1], ids[k]) for k in range(1, QUAD)]
    encs = [
        [remote(enc_ref.at[n], enc_own.at[n, k], enc_ss.at[n, k - 1], enc_rs.at[n, k - 1], ids[k]) for k in range(1, QUAD)]
        for n in range(tiles)
    ]
    srcs = [remote(src_out.at[peers[k]], src_g.at[k - 1], src_ss.at[k - 1], src_rs.at[k - 1], ids[k]) for k in range(1, QUAD)]
    far_encs = [remote(enc_own.at[n], enc_far.at[n], fe_ss.at[n], fe_rs.at[n], pair) for n in range(tiles)]
    far_tgts = [remote(tgt_own.at[k], tgt_far.at[k], ft_ss.at[k], ft_rs.at[k], pair) for k in range(QUAD)]
    stages = [(slice(0, 1), slice(None)), (slice(1, 2), slice(None))]
    stages += [(slice(2, 4), slice(n, n + 1)) for n in range(tiles)]

    def stage_copies(c, s):
        i, n = stages[c]
        rows_to = pl.ds(pl.multiple_of(ring[s] * block, block), block)
        return (
            remote(code.at[i, n, rows_to, :], code_in.at[s - 1, i, n], code_ss.at[c, s - 1], code_rs.at[c, s - 1], ring_ids[s]),
            remote(scale.at[ring[s], i, n], scale_in.at[s - 1, i, n], scale_ss.at[c, s - 1], scale_rs.at[c, s - 1], ring_ids[s]),
        )

    sums = [[copy for s in range(1, groups) for copy in stage_copies(c, s)] for c in range(len(stages))]

    early = tiles // 2
    for copies in (tids, tacts, decs, *encs[:early]):
        for copy in copies:
            copy.start()

    def encode(i, n):
        for g in range(groups):
            at = pl.ds(g * block, block)
            value = part[i, n, at, :]
            size = jnp.abs(value)
            top = jnp.max(size, axis=0, keepdims=True)
            inverse = jnp.where(top > 0, 1.0 / top, 0.0)
            level = (jnp.sqrt(size * inverse) * LEVELS + 0.5).astype(jnp.int32)
            code[i, n, at, :] = jnp.where(value < 0, -level, level).astype(jnp.int16)
            scale[g, i, n] = top * (1.0 / LEVELS**2)

    def put_source(j, h, v):
        per = share // LANES
        src_out[h // per, (h % per) * LANES:(h % per + 1) * LANES, j * rows:(j + 1) * rows] = v.T.astype(BF16)

    build_dense(sid_ref, sact_ref, lo_s, key_s, act_s, tmp, put_source, high)
    for copies in (srcs, *encs[early:]):
        for copy in copies:
            copy.start()

    enc_own[:, 0] = enc_ref[...]
    dec_g[0] = dec_ref[place]

    def put_target(k):
        def put(j, h, v):
            tgt_own[k, j * rows:(j + 1) * rows, h * LANES:(h + 1) * LANES] = v.astype(BF16)

        return put

    def co_add(i, k, target):
        source = src_out[place] if k == 0 else src_g[k - 1]

        @pl.loop(0, tiles)
        def _(n):
            at = pl.ds(pl.multiple_of(n * TILE, TILE), TILE)
            term = jnp.dot(source, target[k, :, at], preferred_element_type=F32)
            if k == 0:
                part[i, n] = term
            else:
                part[i, n] += term
            if k == QUAD - 1:
                encode(i, n)

    depth = QUAD * enc_ref.shape[1]

    def virt(i, n, encoder):
        part[2 + i, n] = jnp.dot(
            dec_t[i], encoder[n].reshape(depth, TILE), preferred_element_type=F32
        )
        encode(2 + i, n)

    build_dense(tid_ref, tact_ref, lo_s, key_s, act_s, tmp, put_target(0), high)
    far_tgts[0].start()
    co_add(0, 0, tgt_own)

    def target_of(k):
        tids[k - 1].wait_recv()
        tacts[k - 1].wait_recv()
        build_dense(tid_g.at[k - 1], tact_g.at[k - 1], lo_s, key_s, act_s, tmp, put_target(k), high)
        far_tgts[k].start()

    target_of(1)
    target_of(2)
    for copy in decs:
        copy.wait_recv()
    for i in range(2):
        dec_t[i] = dec_g[:, i].reshape(depth, share).astype(F32).T.astype(BF16)
    for n in range(early):
        for copy in encs[n]:
            copy.wait_recv()
        far_encs[n].start()
        virt(0, n, enc_own)
        far_encs[n].wait_recv()
        virt(1, n, enc_far)
        for copy in sums[2 + n]:
            copy.start()

    target_of(3)
    for k in range(1, QUAD):
        srcs[k - 1].wait_recv()
        co_add(0, k, tgt_own)
    for copy in sums[0]:
        copy.start()
    for k in range(QUAD):
        far_tgts[k].wait_recv()
        co_add(1, k, tgt_far)
    for copy in sums[1]:
        copy.start()

    for n in range(early, tiles):
        for copy in encs[n]:
            copy.wait_recv()
        far_encs[n].start()
        virt(0, n, enc_own)
        far_encs[n].wait_recv()
        virt(1, n, enc_far)
        for copy in sums[2 + n]:
            copy.start()


    own = pl.ds(pl.multiple_of(group * block, block), block)

    def total(i, n):
        value = part[i, n, own, :]
        for s in range(groups - 1):
            level = code_in[s, i, n].astype(jnp.int32).astype(F32)
            value = value + level * jnp.abs(level) * scale_in[s, i, n]
        return value

    for c in range(2):
        for copy in sums[c]:
            copy.wait_recv()
    for n in range(tiles):
        for copy in sums[2 + n]:
            copy.wait_recv()
        for i, slot in ((0, layer), (1, 1 - layer)):
            out_ref[slot, :, n * TILE:(n + 1) * TILE] = total(2 + i, n) * (total(i, n) * factor)

    for copies in (tids, tacts, decs, *encs, srcs, far_encs, far_tgts, *sums):
        for copy in copies:
            copy.wait_send()


def on_device(src_ids, src_acts, tgt_ids, tgt_acts, enc_cols, dec_rows):
    layer = lax.axis_index("layer")
    shards = lax.axis_size("width")
    groups = shards // QUAD
    count, depth = enc_cols.shape[1:]
    share = count // QUAD
    block = share // groups
    top = src_ids.shape[2] // 2
    tokens = src_ids.shape[1] * 2
    rows, wide = tokens // QUAD, QUAD * top
    factor = (count / top) ** 2 / (tokens * shards)

    def pick(value, index):
        return lax.dynamic_index_in_dim(value, index, 0, False)

    ids = src_ids[0]
    ids = (ids // block % QUAD) * share + ids // (block * QUAD) * block + ids % block
    sid = ids.astype(jnp.int16).reshape(rows, wide)
    sact = src_acts[0].reshape(rows, wide)
    tid = pick(tgt_ids, layer).astype(jnp.int16).reshape(rows, wide)
    tact = pick(tgt_acts, layer).reshape(rows, wide)

    spare = -depth % 16
    enc = jnp.pad(enc_cols[0].T, ((0, spare), (0, 0)))
    dec = dec_rows[0]
    dec = jnp.where(layer == 0, dec, dec[::-1])
    dec = dec.reshape(2, groups, QUAD, block, depth).transpose(2, 0, 4, 1, 3)
    dec = jnp.pad(dec.reshape(QUAD, 2, depth, share), ((0, 0), (0, 0), (0, spare), (0, 0)))
    deep = depth + spare
    tiles = count // TILE
    enc = enc.reshape(deep, tiles, TILE).transpose(1, 0, 2)

    def vmem(*shape, kind=BF16):
        return pltpu.VMEM(shape, kind)

    def sems(*shape):
        return [pltpu.SemaphoreType.DMA(shape)] * 2

    out = pl.pallas_call(
        functools.partial(kernel, groups, factor),
        out_shape=jax.ShapeDtypeStruct((2, block, count), F32),
        in_specs=[pl.BlockSpec(memory_space=pltpu.VMEM)] * 6,
        out_specs=pl.BlockSpec(memory_space=pltpu.VMEM),
        scratch_shapes=[
            vmem(QUAD - 1, rows, wide, kind=jnp.int16),
            vmem(QUAD - 1, rows, wide),
            vmem(tiles, QUAD, deep, TILE),
            vmem(tiles, QUAD, deep, TILE),
            vmem(QUAD, 2, deep, share),
            vmem(QUAD, share, tokens),
            vmem(QUAD - 1, share, tokens),
            vmem(QUAD, tokens, count),
            vmem(QUAD, tokens, count),
            vmem(4, tiles, share, TILE, kind=F32),
            vmem(4, tiles, share, TILE, kind=jnp.int16),
            vmem(groups, 4, tiles, 1, TILE, kind=F32),
            vmem(groups - 1, 4, tiles, block, TILE, kind=jnp.int16),
            vmem(groups - 1, 4, tiles, 1, TILE, kind=F32),
            vmem(2, share, QUAD * deep),
            vmem(rows, wide, kind=F32),
            vmem(rows, wide, kind=F32),
            vmem(rows, wide, kind=F32),
            vmem(rows * (QUAD * (count // LANES) + 8), LANES, kind=F32),
            *sems(QUAD - 1),
            *sems(QUAD - 1),
            *sems(tiles, QUAD - 1),
            *sems(QUAD - 1),
            *sems(QUAD - 1),
            *sems(tiles),
            *sems(QUAD),
            *sems(2 + tiles, groups - 1),
            *sems(2 + tiles, groups - 1),
        ],
        compiler_params=pltpu.CompilerParams(
            collective_id=0, has_side_effects=True, vmem_limit_bytes=56 * 1024 * 1024
        ),
        name="edges",
    )(sid, sact, tid, tact, enc, dec)
    return out[None]


def solution(mesh):
    placed = (
        P("layer", ("parts", "width"), None),
        P("layer", ("parts", "width"), None),
        P(None, ("parts", "width"), None),
        P(None, ("parts", "width"), None),
        P("layer", None, "width"),
        P("layer", None, None, "width"),
    )
    return jax.shard_map(
        on_device,
        mesh=mesh,
        in_specs=placed,
        out_specs=P(("parts", "layer"), None, "width", None),
        check_vma=False,
    )
```
